32 devices in a mesh: sector: 2 (over y), cell: 16 (over z, x, core).
Axes of the slice: x: 2, y: 2, z: 4, core: 2. Of those that a mesh axis runs over, the one named last changes fastest.
Arguments:
- fluid: bfloat16 [2048, 320], P(('sector', 'cell')), may hold values from -10 to 10, as said below
- bead_vel: float32 [512, 3, 128], P(('sector', 'cell')), may hold values from -6 to 6
- bead_diam: float32 [512, 128], P(('sector', 'cell')), may hold values from 0.5 to 2
- weights: bfloat16 [512, 8, 64, 128], P(('sector', 'cell')), may hold values from 0.002 to 1.002, as said below
- tile_owner: int32 [512, 8], P(('sector', 'cell')), may hold values from 0 to 17, all different within a row; in each aligned block of 16 rows (0 to 15, 16 to 31, ...) at most 15 rows name the same one
- tile_local: int32 [512, 8], P(('sector', 'cell')), may hold values from 0 to 63
- tile_count: int32 [512], P(('sector', 'cell')), may hold values from 1 to 8
Outputs:
- bead_drag: float32 [512, 3, 128], P(('sector', 'cell'))
- cell_source: float32 [2048, 192], P(('sector', 'cell'))
The draws below stay inside these ranges and needn't reach their ends.
Inputs may be any that keep to these rules, and one draw needn't show every extreme that they name: `tile_owner`: each row names 8 different owners: below 16 the device of that cell index in the bead block's own angular group, 16 the device of the same cell index in the previous angular group, 17 that in the next (groups wrap around). Among the bead blocks of one device no owner is named by more than 15 rows, a bound that some block reaches. Fields 0 to 2 of each row are velocity components, field 3 the fluid volume fraction in 0.4 to 0.95, field 4 the viscosity in 0.05 to 0.5. Nonnegative kernel weights, each at least 0.002.
All inputs are finite; a program needn't handle non-finite values.
Results may differ from the reference program's by a relative error of at most 0.0023.
Values may be sent and summed in bfloat16 or wider, within the bound.
A program may use at most 64 MiB of HBM per device.

```python
import math
import jax
import jax.numpy as jnp
import numpy as np
from jax import lax

CB_DEV = 64
BB_DEV = 16
KMAX = 8
CELLS = 64
BEADS = 128
FIELDS = 5
CAP = 15
NCB = 2048
NBB = 512
N_SECTOR = 2
N_CELL = 16


def draw_fluid(key, part):
    key = jax.random.fold_in(key, 11)
    key_vel, key_poro, key_visc = jax.random.split(key, 3)
    array_shape = (NCB, FIELDS * CELLS)
    field_index = jax.lax.broadcasted_iota(jnp.int32, array_shape, 1) // CELLS
    velocity = jnp.clip(2.0 * jax.random.normal(key_vel, array_shape, jnp.float32), -10.0, 10.0)
    porosity = jax.random.uniform(key_poro, array_shape, jnp.float32, 0.4, 0.95)
    viscosity = jnp.exp(jax.random.uniform(key_visc, array_shape, jnp.float32, math.log(0.05), math.log(0.5)))
    result = jnp.where(field_index < 3, velocity, jnp.where(field_index == 3, porosity, viscosity))
    return result.astype(jnp.bfloat16)


def draw_weights(key, part):
    key = jax.random.fold_in(key, 23)
    uniform_draw = jax.random.uniform(key, (NBB, KMAX, CELLS, BEADS), jnp.float32)
    result = 0.002 + uniform_draw ** 24
    return result.astype(jnp.bfloat16)


def set_ends(drawn, stream_key, low, top_value):
    place = [jax.random.randint(jax.random.fold_in(stream_key, axis), (), 0, length) for axis, length in enumerate(drawn.shape)]
    main_axis = drawn.shape.index(max(drawn.shape))
    neighbour = place[:main_axis] + [(place[main_axis] + 1) % drawn.shape[main_axis]] + place[main_axis + 1:]
    return drawn.at[tuple(place)].set(low).at[tuple(neighbour)].set(top_value)


def shard_levels(key, dims, cuts, least, top_value):
    def one(axis_at, blocks):
        heights = jax.random.uniform(jax.random.fold_in(jax.random.fold_in(key, 6), axis_at), (blocks,), jnp.float32, least / len(cuts), top_value / len(cuts))
        return jnp.repeat(jnp.exp(heights), dims[axis_at] // blocks).reshape((-1,) + (1,) * (len(dims) - axis_at - 1))

    level = one(*cuts[0])
    for cut in cuts[1:]:
        level = level * one(*cut)
    return level


def assign_block(stream_key, own, number, rows, count, top, most, skew):
    ranking = jax.random.permutation(stream_key, count)
    crowded, usual = load_shares(count, rows * top, most, skew, True), load_shares(count, rows * top, most, skew, False)
    places = jnp.arange(count)

    def named(lengths, turn):
        used = int((lengths > 0).sum())
        fixed = max(1, used // 4)
        passed = fixed + (places - fixed + turn * (used - fixed)) % max(1, count - fixed)
        return jnp.zeros((count,), jnp.int32).at[ranking[jnp.where(places < fixed, places, passed)]].set(jnp.asarray(lengths, jnp.int32))

    lengths = jnp.where(number % 4 == 0, named(crowded, number // 4), named(usual, number - number // 4 - 1))
    mixed = jax.random.permutation(jax.random.fold_in(own, 3), count)
    donor, taker = mixed[0:count // 2 * 2:2], mixed[1:count // 2 * 2:2]
    margin = jnp.minimum(lengths[donor] - 1, most - lengths[taker]) // 2
    margin = jnp.where((donor == ranking[0]) | (taker == ranking[0]) | (lengths[taker] == 0), 0, jnp.maximum(margin, 0))
    passed = jax.random.randint(jax.random.fold_in(own, 4), (count // 2,), 0, 1 << 20) % (margin + 1)
    lengths = lengths.at[donor].add(-passed).at[taker].add(passed)
    items = jnp.searchsorted(jnp.cumsum(lengths), jnp.arange(rows * top), side="right").astype(jnp.int32)
    table = items.reshape(top, rows).T
    table = table[jax.random.permutation(jax.random.fold_in(own, 1), rows)]
    turn = jax.random.randint(jax.random.fold_in(own, 2), (rows, 1), 0, top)
    return jnp.take_along_axis(table, (jnp.arange(top)[None, :] + turn) % top, axis=1)


def load_shares(number_of, total, reach, slope, full):
    loads = [(1 << 20) // math.isqrt(rank ** slope) + 1 for rank in range(1, number_of + 1)]
    largest = reach if full else min(reach, max(-(-total // number_of), total * loads[0] // sum(loads)))
    least = 1 if total - largest >= number_of - 1 else 0
    counts, rest = [largest] + [least] * (number_of - 1), total - largest - least * (number_of - 1)
    while rest > 0:
        free = [i for i in range(1, number_of) if counts[i] < largest] or [i for i in range(1, number_of) if counts[i] < reach]
        pool, left = sum([loads[i] for i in free]), rest
        for i in free:
            extra = min(reach - counts[i], max(1, left * loads[i] // pool), rest)
            counts[i] = counts[i] + extra
            rest = rest - extra
    return np.array(counts)


def noise(key, dims, width, most, shards=(), kind=jnp.bfloat16):
    factor_of = shard_levels(key, dims, shards, -0.22, 0.18) if shards else 1.0
    values = jax.random.normal(key, dims, jnp.float32) * width * factor_of
    return jnp.minimum(jnp.maximum(values, -most), most).astype(kind)


def setup_inputs(seed: int = 0) -> dict:
    seeds = jax.random.split(jax.random.key(seed), 8)
    fluid = draw_fluid(jax.random.fold_in(seeds[7], 71), 0)
    bead_vel = noise(seeds[1], (NBB, 3, BEADS), 1.0, 6.0, ((0, 32),), jnp.float32)
    bead_diam = jnp.clip(jnp.exp(math.log(2.0) - 1.3862944 * jax.random.uniform(seeds[2], (NBB, BEADS), jnp.float32) ** shard_levels(seeds[2], (NBB, BEADS), ((0, 32),), -0.2, 0.2)), 0.5, 2.0)
    weights = draw_weights(jax.random.fold_in(seeds[7], 71), 0)
    tile_owner_keys = jax.random.split(jax.random.fold_in(seeds[4], 1), NBB // BB_DEV)
    tile_owner_turns = jax.random.permutation(jax.random.fold_in(seeds[4], 3), NBB // BB_DEV)
    tile_owner = jax.vmap(lambda own, number: assign_block(jax.random.fold_in(seeds[4], 2), own, number, BB_DEV, N_CELL + 2, KMAX, CAP, 2))(tile_owner_keys, tile_owner_turns).reshape((NBB, KMAX))
    tile_local = set_ends(jax.random.randint(seeds[5], (NBB, KMAX), 0, CB_DEV), jax.random.fold_in(seeds[5], 1), 0, CB_DEV - 1).astype(jnp.int32)
    tile_count = set_ends(jax.random.randint(seeds[6], (NBB,), 1, KMAX + 1), jax.random.fold_in(seeds[6], 1), 1, KMAX).astype(jnp.int32)
    return {"fluid": fluid, "bead_vel": bead_vel, "bead_diam": bead_diam, "weights": weights, "tile_owner": tile_owner, "tile_local": tile_local, "tile_count": tile_count}


def drag_blocks(tile_fluid, weights, bead_vel, bead_diam, live_mask):
    blocks, lists = (weights.shape[0], weights.shape[1])
    fluid_tiles = tile_fluid.reshape(blocks, lists, FIELDS, CELLS).astype(jnp.float32)
    weight_full = weights.astype(jnp.float32)
    tile_vals = jnp.einsum('bkfc,bkcn->bkfn', fluid_tiles, weight_full, precision=lax.Precision.HIGHEST)
    weight_sums = lax.optimization_barrier(jnp.sum(weight_full, axis=2))
    weight_total = lax.optimization_barrier(jnp.sum(live_mask[:, :, None] * weight_sums, axis=1))
    interp = lax.optimization_barrier(jnp.sum(live_mask[:, :, None, None] * tile_vals, axis=1)) / weight_total[:, None, :]
    slip_vel = interp[:, 0:3] - bead_vel
    porosity = interp[:, 3]
    viscosity = interp[:, 4]
    slip_speed = jnp.sqrt(lax.optimization_barrier(jnp.sum(slip_vel * slip_vel, axis=1)) + 0.01)
    reynolds = porosity * bead_diam * slip_speed / viscosity
    drag_coef = viscosity * (1.0 + 0.15 * jnp.power(reynolds, 0.687)) * jnp.power(porosity, -1.65) / (bead_diam * bead_diam)
    bead_drag = drag_coef[:, None, :] * slip_vel
    scaled_drag = (bead_drag / weight_total[:, None, :]).astype(jnp.bfloat16)
    partials = jnp.einsum('bkcn,bjn->bkjc', weight_full, scaled_drag.astype(jnp.float32), precision=lax.Precision.HIGHEST)
    partials = -live_mask[:, :, None, None] * partials
    return (bead_drag, partials)

def reference(fluid, bead_vel, bead_diam, weights, tile_owner, tile_local, tile_count):
    total_blocks = weights.shape[0]
    device_count = total_blocks // BB_DEV
    device = (jnp.arange(total_blocks) // BB_DEV).astype(jnp.int32)
    group_index = device // N_CELL
    cell_index = device % N_CELL
    sector_of = jnp.where(tile_owner == N_CELL, ((group_index - 1) % N_SECTOR)[:, None], jnp.where(tile_owner == N_CELL + 1, ((group_index + 1) % N_SECTOR)[:, None], group_index[:, None]))
    column_of = jnp.where(tile_owner < N_CELL, tile_owner, cell_index[:, None])
    cell_ids = ((sector_of * N_CELL + column_of) * CB_DEV + tile_local).astype(jnp.int32)
    live_mask = (jnp.arange(KMAX)[None, :] < tile_count[:, None]).astype(jnp.float32)

    def per_device(inputs):
        ids_dev, weights_dev, vel_dev, diam_dev, live_dev = inputs
        tile_fluid = fluid[ids_dev]
        return drag_blocks(tile_fluid, weights_dev, vel_dev, diam_dev, live_dev)
    bead_drag, partials = lax.map(per_device, (cell_ids.reshape(device_count, BB_DEV, KMAX), weights.reshape(device_count, BB_DEV, KMAX, CELLS, BEADS), bead_vel.reshape(device_count, BB_DEV, 3, BEADS), bead_diam.reshape(device_count, BB_DEV, BEADS), live_mask.reshape(device_count, BB_DEV, KMAX)))
    bead_drag = bead_drag.reshape(total_blocks, 3, BEADS)
    partials = partials.reshape(total_blocks * KMAX, 3 * CELLS)
    cell_source = jax.ops.segment_sum(partials, cell_ids.reshape(-1), num_segments=fluid.shape[0])
    return (bead_drag, cell_source)
```

```python
import functools

import jax
import jax.numpy as jnp
from jax import lax
from jax.experimental import pallas as pl
from jax.experimental.pallas import tpu as pltpu
from jax.sharding import PartitionSpec as P

FIELDS = 5
MESH = pl.DeviceIdType.MESH


def kernel(
    nsec, ncell, fluid_ref, vel_ref, diam_ref, weights_ref, owner_ref, local_ref, count_ref,
    drag_ref, source_ref,
    w, table, ask, asked, asked_t, reply, rows, lhs, mixed, scaled, parts, give, got,
    w_sem, ask_send, ask_recv, reply_send, reply_recv, give_send, give_recv,
):
    lists = owner_ref.shape[1]
    beads = owner_ref.shape[0]
    cells = fluid_ref.shape[0]
    slots = ncell + 2
    f32, bf16 = jnp.float32, jnp.bfloat16
    me = lax.axis_index("cell")
    sec = lax.axis_index("sector")
    prev = {"sector": lax.rem(sec + nsec - 1, nsec)}
    succ = {"sector": lax.rem(sec + 1, nsec)}
    around = [lax.rem(me + t, ncell) for t in range(1, ncell)]
    to_owner = [(ncell, prev, ncell), (ncell + 1, succ, ncell + 1)]
    to_owner += [(o, {"cell": o}, me) for o in around]
    to_asker = [(ncell, succ, ncell), (ncell + 1, prev, ncell + 1)]
    to_asker += [(o, {"cell": o}, me) for o in around]

    barrier = pltpu.get_barrier_semaphore()
    for _, device, _ in to_owner:
        pl.semaphore_signal(barrier, inc=1, device_id=device, device_id_type=MESH)

    load_w = pltpu.make_async_copy(weights_ref, w, w_sem)
    load_w.start()

    def copy(src, dst, here, device, there, send, recv):
        return pltpu.make_async_remote_copy(
            src_ref=src.at[here], dst_ref=dst.at[there], send_sem=send.at[here],
            recv_sem=recv.at[there], device_id=device, device_id_type=MESH,
        )

    def arrived(src, dst, send, recv, links):
        for slot, device, _ in links:
            copy(src, dst, slot, device, slot, send, recv).wait_recv()

    lane = lax.broadcasted_iota(jnp.int32, (beads, 128), 1)
    square = (beads, beads)
    diagonal = lax.broadcasted_iota(jnp.int32, square, 0) == lax.broadcasted_iota(jnp.int32, square, 1)
    counts = jnp.broadcast_to(count_ref[...].astype(f32), square)
    counts = jnp.sum(jnp.where(diagonal, counts, 0.0), axis=1, keepdims=True)
    turn = lax.broadcasted_iota(jnp.int32, (beads, lists), 1).astype(f32)
    live = turn < counts
    keys = jnp.where(live, owner_ref[...] * 128 + local_ref[...], -1)
    owners = jnp.where(live, owner_ref[...], -1)
    key_of = [jnp.broadcast_to(keys[:, k : k + 1], (beads, 128)) for k in range(lists)]
    owner_of = [jnp.broadcast_to(owners[:, k : k + 1], (beads, 128)) for k in range(lists)]

    for o in range(slots):
        hit = key_of[0] == lane + o * 128
        for k in range(1, lists):
            hit = hit | (key_of[k] == lane + o * 128)
        ask[o] = jnp.where(hit, 1.0, 0.0).astype(bf16)

    pl.semaphore_wait(barrier, len(to_owner))
    asks = [copy(ask, asked, h, d, t, ask_send, ask_recv) for h, d, t in to_owner]
    for c in asks:
        c.start()
    asked[pl.ds(me, 1)] = ask[pl.ds(me, 1)]
    table[...] = jnp.ones_like(table)
    table[:, : FIELDS * cells] = fluid_ref[...]
    lhs[...] = jnp.zeros_like(lhs)
    scaled[...] = jnp.zeros_like(scaled)

    arrived(ask, asked, ask_send, ask_recv, to_owner)
    wanted = asked[...].reshape(slots * beads, 128)
    picked = jnp.dot(wanted[:, :cells], table[...], preferred_element_type=f32)
    reply[...] = picked.astype(bf16).reshape(reply.shape)
    replies = [copy(reply, rows, h, d, t, reply_send, reply_recv) for h, d, t in to_asker]
    for c in replies:
        c.start()
    rows[pl.ds(me, 1)] = reply[pl.ds(me, 1)]
    asked_t[...] = wanted.astype(f32).T.astype(bf16)
    load_w.wait()
    arrived(reply, rows, reply_send, reply_recv, to_asker)

    low = lane < 64
    for c in range(3):
        held = [jnp.zeros((beads, 128), f32) for _ in range(lists)]
        for o in range(slots):
            row = rows[o, :, c * 128 : (c + 1) * 128].astype(f32)
            held = [jnp.where(owner_of[k] == o, row, held[k]) for k in range(lists)]
        for m in range(lists // 2):
            one, two = held[2 * m], held[2 * m + 1]
            even = jnp.where(low, one, pltpu.roll(two, 64, 1))
            odd = jnp.where(low, pltpu.roll(one, 64, 1), two)
            lhs[m, pl.ds(2 * c, beads, stride=8), :] = even
            lhs[m, pl.ds(2 * c + 1, beads, stride=8), :] = odd

    for b in range(beads):
        eight = slice(b * 8, (b + 1) * 8)
        left = jnp.concatenate([lhs[m, eight, :] for m in range(lists // 2)], axis=1)
        mixed[eight, :] = jnp.dot(left.astype(bf16), w[b], preferred_element_type=f32)

    field = [mixed[pl.ds(f, beads, stride=8), :] for f in range(FIELDS + 1)]
    total = field[FIELDS]
    interp = [field[f] / total for f in range(FIELDS)]
    slip = [interp[i] - vel_ref[:, i, :] for i in range(3)]
    porosity, viscosity = interp[3], interp[4]
    diam = diam_ref[...]
    speed = jnp.sqrt(slip[0] * slip[0] + slip[1] * slip[1] + slip[2] * slip[2] + 0.01)
    reynolds = porosity * diam * speed / viscosity
    coef = (
        viscosity
        * (1.0 + 0.15 * jnp.exp(0.687 * jnp.log(reynolds)))
        * jnp.exp(-1.65 * jnp.log(porosity))
        / (diam * diam)
    )
    for i in range(3):
        drag = coef * slip[i]
        drag_ref[:, i, :] = drag
        scaled[pl.ds(i, beads, stride=8), :] = -(drag / total)

    for b in range(beads):
        eight = slice(b * 8, (b + 1) * 8)
        spread = lax.dot_general(
            scaled[eight, :].astype(bf16), w[b],
            (((1,), (1,)), ((), ())), preferred_element_type=f32,
        )
        for m in range(lists // 2):
            parts[m, eight, :] = spread[:, m * 128 : (m + 1) * 128]

    first, second = [None] * lists, [None] * lists
    for m in range(lists // 2):
        g0, g1, g2 = (parts[m, pl.ds(i, beads, stride=8), :] for i in range(3))
        first[2 * m] = jnp.where(low, g0, pltpu.roll(g1, 64, 1))
        first[2 * m + 1] = jnp.where(low, pltpu.roll(g0, 64, 1), g1)
        second[2 * m] = g2
        second[2 * m + 1] = pltpu.roll(g2, 64, 1)

    def fill(slot):
        one, two = jnp.zeros((beads, 128), f32), jnp.zeros((beads, 128), f32)
        for k in range(lists):
            here = owner_of[k] == slot
            one = jnp.where(here, first[k], one)
            two = jnp.where(here, second[k], two)
        both = jnp.concatenate([one, two], axis=1).astype(bf16)
        give[pl.ds(slot, 1)] = both.reshape(1, beads, 256)

    gives = [copy(give, got, h, d, t, give_send, give_recv) for h, d, t in to_owner]
    for c, (slot, _, _) in zip(gives, to_owner):
        fill(slot)
        c.start()
    fill(me)
    got[pl.ds(me, 1)] = give[pl.ds(me, 1)]
    arrived(give, got, give_send, give_recv, to_owner)
    summed = jnp.dot(
        asked_t[...], got[...].reshape(slots * beads, 256), preferred_element_type=f32
    )
    source_ref[...] = summed[:cells, : source_ref.shape[1]]
    for c in asks + replies + gives:
        c.wait_send()


def local(nsec, ncell, fluid, bead_vel, bead_diam, weights, tile_owner, tile_local, tile_count):
    cells_dev, width = fluid.shape
    beads, lists, cells, lanes = weights.shape
    slots = ncell + 2
    f32, bf16 = jnp.float32, jnp.bfloat16
    vmem = pl.BlockSpec(memory_space=pltpu.VMEM)
    dma = pltpu.SemaphoreType.DMA
    return pl.pallas_call(
        functools.partial(kernel, nsec, ncell),
        out_shape=(
            jax.ShapeDtypeStruct(bead_vel.shape, f32),
            jax.ShapeDtypeStruct((cells_dev, 3 * cells), f32),
        ),
        in_specs=[vmem, vmem, vmem, pl.BlockSpec(memory_space=pl.ANY), vmem, vmem, vmem],
        out_specs=(vmem, vmem),
        scratch_shapes=[
            pltpu.VMEM((beads, lists * cells, lanes), bf16),
            pltpu.VMEM((cells_dev, 384), bf16),
            pltpu.VMEM((slots, beads, 128), bf16),
            pltpu.VMEM((slots, beads, 128), bf16),
            pltpu.VMEM((128, slots * beads), bf16),
            pltpu.VMEM((slots, beads, 384), bf16),
            pltpu.VMEM((slots, beads, 384), bf16),
            pltpu.VMEM((lists // 2, beads * 8, 128), f32),
            pltpu.VMEM((beads * 8, lanes), f32),
            pltpu.VMEM((beads * 8, lanes), f32),
            pltpu.VMEM((lists // 2, beads * 8, 128), f32),
            pltpu.VMEM((slots, beads, 256), bf16),
            pltpu.VMEM((slots, beads, 256), bf16),
            dma(()),
            dma((slots,)), dma((slots,)), dma((slots,)),
            dma((slots,)), dma((slots,)), dma((slots,)),
        ],
        compiler_params=pltpu.CompilerParams(
            collective_id=0, has_side_effects=True, vmem_limit_bytes=48 * 1024 * 1024
        ),
    )(
        fluid, bead_vel, bead_diam, weights.reshape(beads, lists * cells, lanes),
        tile_owner, tile_local, tile_count.reshape(1, beads),
    )


def solution(mesh):
    both = ("sector", "cell")
    in_specs = (
        P(both, None), P(both, None, None), P(both, None), P(both, None, None, None),
        P(both, None), P(both, None), P(both),
    )
    out_specs = (P(both, None, None), P(both, None))
    body = functools.partial(local, mesh.shape["sector"], mesh.shape["cell"])
    return jax.shard_map(body, mesh=mesh, in_specs=in_specs, out_specs=out_specs, check_vma=False)
```

```python
import functools

import jax
import jax.numpy as jnp
from jax import lax
from jax.experimental import pallas as pl
from jax.experimental.pallas import tpu as pltpu
from jax.sharding import PartitionSpec as P

FIELDS = 5
MESH = pl.DeviceIdType.MESH


def kernel(
    nsec, ncell, fluid_ref, vel_ref, diam_ref, weights_ref, owner_ref, local_ref, count_ref,
    drag_ref, source_ref,
    fluid, vel, diam, owner, place, count, drags, source,
    w, table, ask, asked, asked_t, reply, rows, lhs, mixed, scaled, parts, give, got,
    in_sem, out_sem, ask_send, ask_recv, reply_send, reply_recv, give_send, give_recv,
):
    lists, beads = owner_ref.shape
    cells = fluid_ref.shape[0]
    slots = ncell + 2
    f32, bf16 = jnp.float32, jnp.bfloat16
    me = lax.axis_index("cell")
    sec = lax.axis_index("sector")
    prev = {"sector": lax.rem(sec + nsec - 1, nsec)}
    succ = {"sector": lax.rem(sec + 1, nsec)}
    around = [lax.rem(me + t, ncell) for t in range(1, ncell)]
    to_owner = [(ncell, prev, ncell), (ncell + 1, succ, ncell + 1)]
    to_owner += [(o, {"cell": o}, me) for o in around]
    to_asker = [(ncell, succ, ncell), (ncell + 1, prev, ncell + 1)]
    to_asker += [(o, {"cell": o}, me) for o in around]

    barrier = pltpu.get_barrier_semaphore()
    for _, device, _ in to_owner:
        pl.semaphore_signal(barrier, inc=1, device_id=device, device_id_type=MESH)

    inputs = [
        (owner_ref, owner), (local_ref, place), (count_ref, count), (fluid_ref, fluid),
        (vel_ref, vel), (diam_ref, diam), (weights_ref, w),
    ]
    loads = [pltpu.make_async_copy(src, dst, in_sem.at[i]) for i, (src, dst) in enumerate(inputs)]
    for c in loads:
        c.start()

    def copy(src, dst, here, device, there, send, recv):
        return pltpu.make_async_remote_copy(
            src_ref=src.at[here], dst_ref=dst.at[there], send_sem=send.at[here],
            recv_sem=recv.at[there], device_id=device, device_id_type=MESH,
        )

    def arrived(src, dst, send, recv, links):
        for slot, device, _ in links:
            copy(src, dst, slot, device, slot, send, recv).wait_recv()

    lane = lax.broadcasted_iota(jnp.int32, (beads, 128), 1)
    ask[...] = jnp.full_like(ask, -1.0)
    for c in loads[:3]:
        c.wait()
    live = lax.broadcasted_iota(jnp.int32, (lists, beads), 0) < count[...]
    owners = jnp.where(live, owner[...], -1).astype(f32)
    places = place[...].astype(f32)
    for o in range(slots):
        ask[o, :, :beads] = jnp.max(jnp.where(owners == o, places, -1.0), axis=0, keepdims=True)

    pl.semaphore_wait(barrier, len(to_owner))
    asks = [copy(ask, asked, h, d, t, ask_send, ask_recv) for h, d, t in to_owner]
    for c in asks:
        c.start()
    asked[pl.ds(me, 1)] = ask[pl.ds(me, 1)]
    diagonal = lane == lax.broadcasted_iota(jnp.int32, (beads, 128), 0)
    lanes = lane.astype(f32)

    def upright(row):
        spread = jnp.where(diagonal[:, : row.shape[1]], jnp.broadcast_to(row, (beads, row.shape[1])), 0.0)
        return jnp.broadcast_to(jnp.sum(spread, axis=1, keepdims=True), (beads, 128))

    owner_of = [upright(owners[k : k + 1, :]) for k in range(lists)]
    loads[3].wait()
    table[...] = jnp.ones_like(table)
    table[:, : FIELDS * cells] = fluid[...]
    lhs[...] = jnp.zeros_like(lhs)
    scaled[...] = jnp.zeros_like(scaled)

    arrived(ask, asked, ask_send, ask_recv, to_owner)
    wanted = jnp.concatenate(
        [jnp.where(upright(asked[o]) == lanes, 1.0, 0.0) for o in range(slots)], axis=0
    )
    picked = jnp.dot(wanted.astype(bf16)[:, :cells], table[...], preferred_element_type=f32)
    reply[...] = picked.astype(bf16).reshape(reply.shape)
    replies = [copy(reply, rows, h, d, t, reply_send, reply_recv) for h, d, t in to_asker]
    for c in replies:
        c.start()
    rows[pl.ds(me, 1)] = reply[pl.ds(me, 1)]
    asked_t[...] = wanted.T.astype(bf16)
    for c in loads[4:]:
        c.wait()
    arrived(reply, rows, reply_send, reply_recv, to_asker)

    low = lane < 64
    for c in range(3):
        held = [jnp.zeros((beads, 128), f32) for _ in range(lists)]
        for o in range(slots):
            row = rows[o, :, c * 128 : (c + 1) * 128].astype(f32)
            held = [jnp.where(owner_of[k] == o, row, held[k]) for k in range(lists)]
        for m in range(lists // 2):
            one, two = held[2 * m], held[2 * m + 1]
            even = jnp.where(low, one, pltpu.roll(two, 64, 1))
            odd = jnp.where(low, pltpu.roll(one, 64, 1), two)
            lhs[m, pl.ds(2 * c, beads, stride=8), :] = even
            lhs[m, pl.ds(2 * c + 1, beads, stride=8), :] = odd

    for b in range(beads):
        eight = slice(b * 8, (b + 1) * 8)
        left = jnp.concatenate([lhs[m, eight, :] for m in range(lists // 2)], axis=1)
        mixed[eight, :] = jnp.dot(left.astype(bf16), w[b], preferred_element_type=f32)

    field = [mixed[pl.ds(f, beads, stride=8), :] for f in range(FIELDS + 1)]
    total = field[FIELDS]
    interp = [field[f] / total for f in range(FIELDS)]
    slip = [interp[i] - vel[i] for i in range(3)]
    porosity, viscosity = interp[3], interp[4]
    across = diam[...]
    speed = jnp.sqrt(slip[0] * slip[0] + slip[1] * slip[1] + slip[2] * slip[2] + 0.01)
    reynolds = porosity * across * speed / viscosity
    coef = (
        viscosity
        * (1.0 + 0.15 * jnp.exp(0.687 * jnp.log(reynolds)))
        * jnp.exp(-1.65 * jnp.log(porosity))
        / (across * across)
    )
    for i in range(3):
        drag = coef * slip[i]
        drags[i] = drag
        scaled[pl.ds(i, beads, stride=8), :] = -(drag / total)

    store_drag = pltpu.make_async_copy(drags, drag_ref, out_sem.at[0])
    store_drag.start()
    for b in range(beads):
        eight = slice(b * 8, (b + 1) * 8)
        spread = lax.dot_general(
            scaled[eight, :].astype(bf16), w[b],
            (((1,), (1,)), ((), ())), preferred_element_type=f32,
        )
        for m in range(lists // 2):
            parts[m, eight, :] = spread[:, m * 128 : (m + 1) * 128]

    first, second = [None] * lists, [None] * lists
    for m in range(lists // 2):
        g0, g1, g2 = (parts[m, pl.ds(i, beads, stride=8), :] for i in range(3))
        first[2 * m] = jnp.where(low, g0, pltpu.roll(g1, 64, 1))
        first[2 * m + 1] = jnp.where(low, pltpu.roll(g0, 64, 1), g1)
        second[2 * m] = g2
        second[2 * m + 1] = pltpu.roll(g2, 64, 1)

    def fill(slot):
        one, two = jnp.zeros((beads, 128), f32), jnp.zeros((beads, 128), f32)
        for k in range(lists):
            here = owner_of[k] == slot
            one = jnp.where(here, first[k], one)
            two = jnp.where(here, second[k], two)
        both = jnp.concatenate([one, two], axis=1).astype(bf16)
        give[pl.ds(slot, 1)] = both.reshape(1, beads, 256)

    gives = [copy(give, got, h, d, t, give_send, give_recv) for h, d, t in to_owner]
    for c, (slot, _, _) in zip(gives, to_owner):
        fill(slot)
        c.start()
    fill(me)
    got[pl.ds(me, 1)] = give[pl.ds(me, 1)]
    arrived(give, got, give_send, give_recv, to_owner)
    summed = jnp.dot(
        asked_t[...], got[...].reshape(slots * beads, 256), preferred_element_type=f32
    )
    source[...] = summed[:cells, : source_ref.shape[1]]
    store_source = pltpu.make_async_copy(source, source_ref, out_sem.at[1])
    store_source.start()
    for c in asks + replies + gives:
        c.wait_send()
    store_drag.wait()
    store_source.wait()


def local(nsec, ncell, fluid, bead_vel, bead_diam, weights, tile_owner, tile_local, tile_count):
    cells_dev, width = fluid.shape
    beads, lists, cells, lanes = weights.shape
    slots = ncell + 2
    f32, bf16, i32 = jnp.float32, jnp.bfloat16, jnp.int32
    hbm = pl.BlockSpec(memory_space=pltpu.HBM)
    dma = pltpu.SemaphoreType.DMA
    drag, source = pl.pallas_call(
        functools.partial(kernel, nsec, ncell),
        out_shape=(
            jax.ShapeDtypeStruct((3, beads, lanes), f32),
            jax.ShapeDtypeStruct((cells_dev, 3 * cells), f32),
        ),
        in_specs=[hbm] * 7,
        out_specs=(hbm, hbm),
        scratch_shapes=[
            pltpu.VMEM((cells_dev, width), bf16),
            pltpu.VMEM((3, beads, lanes), f32),
            pltpu.VMEM((beads, lanes), f32),
            pltpu.VMEM((lists, beads), i32),
            pltpu.VMEM((lists, beads), i32),
            pltpu.VMEM((1, beads), i32),
            pltpu.VMEM((3, beads, lanes), f32),
            pltpu.VMEM((cells_dev, 3 * cells), f32),
            pltpu.VMEM((beads, lists * cells, lanes), bf16),
            pltpu.VMEM((cells_dev, 384), bf16),
            pltpu.VMEM((slots, 1, 128), f32),
            pltpu.VMEM((slots, 1, 128), f32),
            pltpu.VMEM((128, slots * beads), bf16),
            pltpu.VMEM((slots, beads, 384), bf16),
            pltpu.VMEM((slots, beads, 384), bf16),
            pltpu.VMEM((lists // 2, beads * 8, 128), f32),
            pltpu.VMEM((beads * 8, lanes), f32),
            pltpu.VMEM((beads * 8, lanes), f32),
            pltpu.VMEM((lists // 2, beads * 8, 128), f32),
            pltpu.VMEM((slots, beads, 256), bf16),
            pltpu.VMEM((slots, beads, 256), bf16),
            dma((7,)), dma((2,)),
            dma((slots,)), dma((slots,)), dma((slots,)),
            dma((slots,)), dma((slots,)), dma((slots,)),
        ],
        compiler_params=pltpu.CompilerParams(
            collective_id=0, has_side_effects=True, vmem_limit_bytes=60 * 1024 * 1024
        ),
    )(
        fluid, bead_vel.transpose(1, 0, 2), bead_diam,
        weights.reshape(beads, lists * cells, lanes),
        tile_owner.T, tile_local.T, tile_count.reshape(1, beads),
    )
    return drag.transpose(1, 0, 2), source


def solution(mesh):
    both = ("sector", "cell")
    in_specs = (
        P(both, None), P(both, None, None), P(both, None), P(both, None, None, None),
        P(both, None), P(both, None), P(both),
    )
    out_specs = (P(both, None, None), P(both, None))
    body = functools.partial(local, mesh.shape["sector"], mesh.shape["cell"])
    return jax.shard_map(body, mesh=mesh, in_specs=in_specs, out_specs=out_specs, check_vma=False)
```

```python
import functools

import jax
import jax.numpy as jnp
from jax import lax
from jax.experimental import pallas as pl
from jax.experimental.pallas import tpu as pltpu
from jax.sharding import PartitionSpec as P

FIELDS = 5
MESH = pl.DeviceIdType.MESH


def kernel(
    nsec, ncell, fluid_ref, vel_ref, diam_ref, weights_ref, owner_ref, local_ref, count_ref,
    drag_ref, source_ref,
    fluid, vel, diam, owner, place, count, drags, source,
    w, table, ask, asked, asked_t, reply, rows, lhs, mixed, scaled, parts, give, got,
    in_sem, out_sem, ask_send, ask_recv, reply_send, reply_recv, give_send, give_recv,
):
    lists, beads = owner_ref.shape
    cells = fluid_ref.shape[0]
    slots = ncell + 2
    f32, bf16 = jnp.float32, jnp.bfloat16
    me = lax.axis_index("cell")
    sec = lax.axis_index("sector")
    prev = {"sector": lax.rem(sec + nsec - 1, nsec)}
    succ = {"sector": lax.rem(sec + 1, nsec)}
    around = [lax.rem(me + t, ncell) for t in range(1, ncell)]
    to_owner = [(ncell, prev, ncell), (ncell + 1, succ, ncell + 1)]
    to_owner += [(o, {"cell": o}, me) for o in around]
    to_asker = [(ncell, succ, ncell), (ncell + 1, prev, ncell + 1)]
    to_asker += [(o, {"cell": o}, me) for o in around]

    barrier = pltpu.get_barrier_semaphore()
    for _, device, _ in to_owner:
        pl.semaphore_signal(barrier, inc=1, device_id=device, device_id_type=MESH)

    inputs = [
        (owner_ref, owner), (local_ref, place), (count_ref, count), (fluid_ref, fluid),
        (vel_ref, vel), (diam_ref, diam), (weights_ref, w),
    ]
    loads = [pltpu.make_async_copy(src, dst, in_sem.at[i]) for i, (src, dst) in enumerate(inputs)]
    for c in loads:
        c.start()

    def copy(src, dst, here, device, there, send, recv):
        return pltpu.make_async_remote_copy(
            src_ref=src.at[here], dst_ref=dst.at[there], send_sem=send.at[here],
            recv_sem=recv.at[there], device_id=device, device_id_type=MESH,
        )

    def arrived(src, dst, send, recv, links):
        for slot, device, _ in links:
            copy(src, dst, slot, device, slot, send, recv).wait_recv()

    lane = lax.broadcasted_iota(jnp.int32, (beads, 128), 1)
    ask[...] = jnp.full_like(ask, -1.0)
    for c in loads[:3]:
        c.wait()
    live = lax.broadcasted_iota(jnp.int32, (lists, beads), 0) < count[...]
    owners = jnp.where(live, owner[...], -1).astype(f32)
    places = place[...].astype(f32)
    for o in range(slots):
        ask[o, :, :beads] = jnp.max(jnp.where(owners == o, places, -1.0), axis=0, keepdims=True)

    pl.semaphore_wait(barrier, len(to_owner))
    asks = [copy(ask, asked, h, d, t, ask_send, ask_recv) for h, d, t in to_owner]
    for c in asks:
        c.start()
    asked[pl.ds(me, 1)] = ask[pl.ds(me, 1)]
    diagonal = lane == lax.broadcasted_iota(jnp.int32, (beads, 128), 0)
    lanes = lane.astype(f32)

    def upright(row):
        spread = jnp.where(diagonal[:, : row.shape[1]], jnp.broadcast_to(row, (beads, row.shape[1])), 0.0)
        return jnp.broadcast_to(jnp.sum(spread, axis=1, keepdims=True), (beads, 128))

    owner_of = [upright(owners[k : k + 1, :]) for k in range(lists)]
    loads[3].wait()
    table[...] = jnp.ones_like(table)
    table[:, : FIELDS * cells] = fluid[...]
    lhs[...] = jnp.zeros_like(lhs)
    scaled[...] = jnp.zeros_like(scaled)

    arrived(ask, asked, ask_send, ask_recv, to_owner)
    wanted = jnp.concatenate(
        [jnp.where(upright(asked[o]) == lanes, 1.0, 0.0) for o in range(slots)], axis=0
    )
    picked = jnp.dot(wanted.astype(bf16)[:, :cells], table[...], preferred_element_type=f32)
    reply[...] = picked.astype(bf16).reshape(reply.shape)
    replies = [copy(reply, rows, h, d, t, reply_send, reply_recv) for h, d, t in to_asker]
    for c in replies:
        c.start()
    rows[pl.ds(me, 1)] = reply[pl.ds(me, 1)]
    asked_t[...] = wanted.T.astype(bf16)
    for c in loads[4:]:
        c.wait()
    arrived(reply, rows, reply_send, reply_recv, to_asker)

    low = lane < 64
    for c in range(3):
        held = [jnp.zeros((beads, 128), f32) for _ in range(lists)]
        for o in range(slots):
            row = rows[o, :, c * 128 : (c + 1) * 128].astype(f32)
            held = [jnp.where(owner_of[k] == o, row, held[k]) for k in range(lists)]
        for m in range(lists // 2):
            one, two = held[2 * m], held[2 * m + 1]
            even = jnp.where(low, one, pltpu.roll(two, 64, 1))
            odd = jnp.where(low, pltpu.roll(one, 64, 1), two)
            lhs[m, pl.ds(2 * c, beads, stride=8), :] = even
            lhs[m, pl.ds(2 * c + 1, beads, stride=8), :] = odd

    for b in range(beads):
        eight = slice(b * 8, (b + 1) * 8)
        left = jnp.concatenate([lhs[m, eight, :] for m in range(lists // 2)], axis=1)
        mixed[eight, :] = jnp.dot(left.astype(bf16), w[b], preferred_element_type=f32)

    field = [mixed[pl.ds(f, beads, stride=8), :] for f in range(FIELDS + 1)]
    total = field[FIELDS]
    interp = [field[f] / total for f in range(FIELDS)]
    slip = [interp[i] - vel[i] for i in range(3)]
    porosity, viscosity = interp[3], interp[4]
    across = diam[...]
    speed = jnp.sqrt(slip[0] * slip[0] + slip[1] * slip[1] + slip[2] * slip[2] + 0.01)
    reynolds = porosity * across * speed / viscosity
    coef = (
        viscosity
        * (1.0 + 0.15 * jnp.exp(0.687 * jnp.log(reynolds)))
        * jnp.exp(-1.65 * jnp.log(porosity))
        / (across * across)
    )
    for i in range(3):
        drag = coef * slip[i]
        drags[i] = drag
        scaled[pl.ds(i, beads, stride=8), :] = -(drag / total)

    store_drag = pltpu.make_async_copy(drags, drag_ref, out_sem.at[0])
    store_drag.start()
    for b in range(beads):
        eight = slice(b * 8, (b + 1) * 8)
        spread = lax.dot_general(
            scaled[eight, :].astype(bf16), w[b],
            (((1,), (1,)), ((), ())), preferred_element_type=f32,
        )
        for m in range(lists // 2):
            parts[m, eight, :] = spread[:, m * 128 : (m + 1) * 128]

    first, second = [None] * lists, [None] * lists
    for m in range(lists // 2):
        g0, g1, g2 = (parts[m, pl.ds(i, beads, stride=8), :] for i in range(3))
        first[2 * m] = jnp.where(low, g0, pltpu.roll(g1, 64, 1))
        first[2 * m + 1] = jnp.where(low, pltpu.roll(g0, 64, 1), g1)
        second[2 * m] = g2
        second[2 * m + 1] = pltpu.roll(g2, 64, 1)

    def fill(slot):
        one, two = jnp.zeros((beads, 128), f32), jnp.zeros((beads, 128), f32)
        for k in range(lists):
            here = owner_of[k] == slot
            one = jnp.where(here, first[k], one)
            two = jnp.where(here, second[k], two)
        both = jnp.concatenate([one, two], axis=1).astype(bf16)
        give[pl.ds(slot, 1)] = both.reshape(1, beads, 256)

    gives = [copy(give, got, h, d, t, give_send, give_recv) for h, d, t in to_owner]
    for c, (slot, _, _) in zip(gives, to_owner):
        fill(slot)
        c.start()
    fill(me)
    got[pl.ds(me, 1)] = give[pl.ds(me, 1)]
    arrived(give, got, give_send, give_recv, to_owner)
    summed = jnp.dot(
        asked_t[...], got[...].reshape(slots * beads, 256), preferred_element_type=f32
    )
    source[...] = summed[:cells, : source_ref.shape[1]]
    store_source = pltpu.make_async_copy(source, source_ref, out_sem.at[1])
    store_source.start()
    for c in asks + replies + gives:
        c.wait_send()
    store_drag.wait()
    store_source.wait()


def hand_over(drag_ref, source_ref, drag_out, source_out):
    drag_out[...] = drag_ref[...]
    source_out[...] = source_ref[...]


def local(nsec, ncell, fluid, bead_vel, bead_diam, weights, tile_owner, tile_local, tile_count):
    cells_dev, width = fluid.shape
    beads, lists, cells, lanes = weights.shape
    slots = ncell + 2
    f32, bf16, i32 = jnp.float32, jnp.bfloat16, jnp.int32
    hbm = pl.BlockSpec(memory_space=pltpu.HBM)
    vmem = pl.BlockSpec(memory_space=pltpu.VMEM)
    dma = pltpu.SemaphoreType.DMA
    drag, source = pl.pallas_call(
        functools.partial(kernel, nsec, ncell),
        out_shape=(
            jax.ShapeDtypeStruct((3, beads, lanes), f32),
            jax.ShapeDtypeStruct((cells_dev, 3 * cells), f32),
        ),
        in_specs=[hbm] * 7,
        out_specs=(hbm, hbm),
        scratch_shapes=[
            pltpu.VMEM((cells_dev, width), bf16),
            pltpu.VMEM((3, beads, lanes), f32),
            pltpu.VMEM((beads, lanes), f32),
            pltpu.VMEM((lists, beads), i32),
            pltpu.VMEM((lists, beads), i32),
            pltpu.VMEM((1, beads), i32),
            pltpu.VMEM((3, beads, lanes), f32),
            pltpu.VMEM((cells_dev, 3 * cells), f32),
            pltpu.VMEM((beads, lists * cells, lanes), bf16),
            pltpu.VMEM((cells_dev, 384), bf16),
            pltpu.VMEM((slots, 1, 128), f32),
            pltpu.VMEM((slots, 1, 128), f32),
            pltpu.VMEM((128, slots * beads), bf16),
            pltpu.VMEM((slots, beads, 384), bf16),
            pltpu.VMEM((slots, beads, 384), bf16),
            pltpu.VMEM((lists // 2, beads * 8, 128), f32),
            pltpu.VMEM((beads * 8, lanes), f32),
            pltpu.VMEM((beads * 8, lanes), f32),
            pltpu.VMEM((lists // 2, beads * 8, 128), f32),
            pltpu.VMEM((slots, beads, 256), bf16),
            pltpu.VMEM((slots, beads, 256), bf16),
            dma((7,)), dma((2,)),
            dma((slots,)), dma((slots,)), dma((slots,)),
            dma((slots,)), dma((slots,)), dma((slots,)),
        ],
        compiler_params=pltpu.CompilerParams(
            collective_id=0, has_side_effects=True, vmem_limit_bytes=60 * 1024 * 1024
        ),
    )(
        fluid, bead_vel.transpose(1, 0, 2), bead_diam,
        weights.reshape(beads, lists * cells, lanes),
        tile_owner.T, tile_local.T, tile_count.reshape(1, beads),
    )
    drag, source = pl.pallas_call(
        hand_over,
        out_shape=(
            jax.ShapeDtypeStruct(drag.shape, f32), jax.ShapeDtypeStruct(source.shape, f32),
        ),
        in_specs=[vmem] * 2,
        out_specs=(vmem, vmem),
        compiler_params=pltpu.CompilerParams(vmem_limit_bytes=60 * 1024 * 1024),
    )(drag, source)
    return drag.transpose(1, 0, 2), source


def solution(mesh):
    both = ("sector", "cell")
    in_specs = (
        P(both, None), P(both, None, None), P(both, None), P(both, None, None, None),
        P(both, None), P(both, None), P(both),
    )
    out_specs = (P(both, None, None), P(both, None))
    body = functools.partial(local, mesh.shape["sector"], mesh.shape["cell"])
    return jax.shard_map(body, mesh=mesh, in_specs=in_specs, out_specs=out_specs, check_vma=False)
```

```python
import functools

import jax
import jax.numpy as jnp
from jax import lax
from jax.experimental import pallas as pl
from jax.experimental.pallas import tpu as pltpu
from jax.sharding import PartitionSpec as P

FIELDS = 5
MESH = pl.DeviceIdType.MESH


def kernel(
    nsec, ncell, fluid_ref, vel_ref, diam_ref, weights_ref, owner_ref, local_ref, count_ref,
    drag_ref, source_ref,
    fluid, vel, diam, owner, place, count, drags, source,
    w, table, ask, asked, asked_t, reply, rows, lhs, mixed, scaled, parts, give, got,
    in_sem, out_sem, ask_send, ask_recv, reply_send, reply_recv, give_send, give_recv,
):
    lists, beads = owner_ref.shape
    cells = fluid_ref.shape[0]
    slots = ncell + 2
    f32, bf16 = jnp.float32, jnp.bfloat16
    me = lax.axis_index("cell")
    sec = lax.axis_index("sector")
    prev = {"sector": lax.rem(sec + nsec - 1, nsec)}
    succ = {"sector": lax.rem(sec + 1, nsec)}
    around = [lax.rem(me + t, ncell) for t in range(1, ncell)]
    to_owner = [(ncell, prev, ncell), (ncell + 1, succ, ncell + 1)]
    to_owner += [(o, {"cell": o}, me) for o in around]
    to_asker = [(ncell, succ, ncell), (ncell + 1, prev, ncell + 1)]
    to_asker += [(o, {"cell": o}, me) for o in around]

    barrier = pltpu.get_barrier_semaphore()
    for _, device, _ in to_owner:
        pl.semaphore_signal(barrier, inc=1, device_id=device, device_id_type=MESH)

    inputs = [
        (owner_ref, owner), (local_ref, place), (count_ref, count), (fluid_ref, fluid),
        (vel_ref, vel), (diam_ref, diam), (weights_ref, w),
    ]
    loads = [pltpu.make_async_copy(src, dst, in_sem.at[i]) for i, (src, dst) in enumerate(inputs)]
    for c in loads:
        c.start()

    def copy(src, dst, here, device, there, send, recv):
        return pltpu.make_async_remote_copy(
            src_ref=src.at[here], dst_ref=dst.at[there], send_sem=send.at[here],
            recv_sem=recv.at[there], device_id=device, device_id_type=MESH,
        )

    def arrived(src, dst, send, recv, links):
        for slot, device, _ in links:
            copy(src, dst, slot, device, slot, send, recv).wait_recv()

    lane = lax.broadcasted_iota(jnp.int32, (beads, 128), 1)
    ask[...] = jnp.full_like(ask, -1.0)
    for c in loads[:3]:
        c.wait()
    live = lax.broadcasted_iota(jnp.int32, (lists, beads), 0) < count[...]
    owners = jnp.where(live, owner[...], -1).astype(f32)
    places = place[...].astype(f32)
    for o in range(slots):
        ask[o, :, :beads] = jnp.max(jnp.where(owners == o, places, -1.0), axis=0, keepdims=True)

    pl.semaphore_wait(barrier, len(to_owner))
    asks = [copy(ask, asked, h, d, t, ask_send, ask_recv) for h, d, t in to_owner]
    for c in asks:
        c.start()
    asked[pl.ds(me, 1)] = ask[pl.ds(me, 1)]
    diagonal = lane == lax.broadcasted_iota(jnp.int32, (beads, 128), 0)
    lanes = lane.astype(f32)

    def upright(row):
        spread = jnp.where(diagonal[:, : row.shape[1]], jnp.broadcast_to(row, (beads, row.shape[1])), 0.0)
        return jnp.broadcast_to(jnp.sum(spread, axis=1, keepdims=True), (beads, 128))

    owner_of = [upright(owners[k : k + 1, :]) for k in range(lists)]
    loads[3].wait()
    table[...] = jnp.ones_like(table)
    table[:, : FIELDS * cells] = fluid[...]
    lhs[...] = jnp.zeros_like(lhs)
    scaled[...] = jnp.zeros_like(scaled)

    behind = [lax.rem(me + ncell - t, ncell) for t in range(1, ncell)]
    near = [(o, {"cell": o}, me) for o in behind[: ncell // 2]]
    far = [(o, {"cell": o}, me) for o in behind[ncell // 2 :]]
    rim = [(ncell, succ, ncell), (ncell + 1, prev, ncell + 1)]

    def answer(links, own):
        arrived(ask, asked, ask_send, ask_recv, links)
        froms = own + [slot for slot, _, _ in links]
        sought = jnp.concatenate(
            [jnp.where(upright(asked[o]) == lanes, 1.0, 0.0) for o in froms], axis=0
        )
        picked = jnp.dot(sought.astype(bf16)[:, :cells], table[...], preferred_element_type=f32)
        picked = picked.astype(bf16)
        sent = []
        for n, slot in enumerate(froms):
            block = picked[n * beads : (n + 1) * beads].reshape(1, beads, 384)
            reply[pl.ds(slot, 1)] = block
            if n >= len(own):
                _, device, there = links[n - len(own)]
                sent.append(copy(reply, rows, slot, device, there, reply_send, reply_recv))
                sent[-1].start()
        return sent

    replies = answer(near + rim, [me]) + answer(far, [])
    rows[pl.ds(me, 1)] = reply[pl.ds(me, 1)]
    wanted = jnp.concatenate(
        [jnp.where(upright(asked[o]) == lanes, 1.0, 0.0) for o in range(slots)], axis=0
    )
    asked_t[...] = wanted.T.astype(bf16)
    for c in loads[4:]:
        c.wait()
    arrived(reply, rows, reply_send, reply_recv, to_asker)

    low = lane < 64
    for c in range(3):
        held = [jnp.zeros((beads, 128), f32) for _ in range(lists)]
        for o in range(slots):
            row = rows[o, :, c * 128 : (c + 1) * 128].astype(f32)
            held = [jnp.where(owner_of[k] == o, row, held[k]) for k in range(lists)]
        for m in range(lists // 2):
            one, two = held[2 * m], held[2 * m + 1]
            even = jnp.where(low, one, pltpu.roll(two, 64, 1))
            odd = jnp.where(low, pltpu.roll(one, 64, 1), two)
            lhs[m, pl.ds(2 * c, beads, stride=8), :] = even
            lhs[m, pl.ds(2 * c + 1, beads, stride=8), :] = odd

    for b in range(beads):
        eight = slice(b * 8, (b + 1) * 8)
        left = jnp.concatenate([lhs[m, eight, :] for m in range(lists // 2)], axis=1)
        mixed[eight, :] = jnp.dot(left.astype(bf16), w[b], preferred_element_type=f32)

    field = [mixed[pl.ds(f, beads, stride=8), :] for f in range(FIELDS + 1)]
    total = field[FIELDS]
    interp = [field[f] / total for f in range(FIELDS)]
    slip = [interp[i] - vel[i] for i in range(3)]
    porosity, viscosity = interp[3], interp[4]
    across = diam[...]
    speed = jnp.sqrt(slip[0] * slip[0] + slip[1] * slip[1] + slip[2] * slip[2] + 0.01)
    reynolds = porosity * across * speed / viscosity
    coef = (
        viscosity
        * (1.0 + 0.15 * jnp.exp(0.687 * jnp.log(reynolds)))
        * jnp.exp(-1.65 * jnp.log(porosity))
        / (across * across)
    )
    for i in range(3):
        drag = coef * slip[i]
        drags[i] = drag
        scaled[pl.ds(i, beads, stride=8), :] = -(drag / total)

    store_drag = pltpu.make_async_copy(drags, drag_ref, out_sem.at[0])
    store_drag.start()
    for b in range(beads):
        eight = slice(b * 8, (b + 1) * 8)
        spread = lax.dot_general(
            scaled[eight, :].astype(bf16), w[b],
            (((1,), (1,)), ((), ())), preferred_element_type=f32,
        )
        for m in range(lists // 2):
            parts[m, eight, :] = spread[:, m * 128 : (m + 1) * 128]

    first, second = [None] * lists, [None] * lists
    for m in range(lists // 2):
        g0, g1, g2 = (parts[m, pl.ds(i, beads, stride=8), :] for i in range(3))
        first[2 * m] = jnp.where(low, g0, pltpu.roll(g1, 64, 1))
        first[2 * m + 1] = jnp.where(low, pltpu.roll(g0, 64, 1), g1)
        second[2 * m] = g2
        second[2 * m + 1] = pltpu.roll(g2, 64, 1)

    def fill(slot):
        one, two = jnp.zeros((beads, 128), f32), jnp.zeros((beads, 128), f32)
        for k in range(lists):
            here = owner_of[k] == slot
            one = jnp.where(here, first[k], one)
            two = jnp.where(here, second[k], two)
        both = jnp.concatenate([one, two], axis=1).astype(bf16)
        give[pl.ds(slot, 1)] = both.reshape(1, beads, 256)

    gives = [copy(give, got, h, d, t, give_send, give_recv) for h, d, t in to_owner]
    for c, (slot, _, _) in zip(gives, to_owner):
        fill(slot)
        c.start()
    fill(me)
    got[pl.ds(me, 1)] = give[pl.ds(me, 1)]
    arrived(give, got, give_send, give_recv, to_owner)
    summed = jnp.dot(
        asked_t[...], got[...].reshape(slots * beads, 256), preferred_element_type=f32
    )
    source[...] = summed[:cells, : source_ref.shape[1]]
    store_source = pltpu.make_async_copy(source, source_ref, out_sem.at[1])
    store_source.start()
    for c in asks + replies + gives:
        c.wait_send()
    store_drag.wait()
    store_source.wait()


def hand_over(drag_ref, source_ref, drag_out, source_out):
    drag_out[...] = drag_ref[...]
    source_out[...] = source_ref[...]


def local(nsec, ncell, fluid, bead_vel, bead_diam, weights, tile_owner, tile_local, tile_count):
    cells_dev, width = fluid.shape
    beads, lists, cells, lanes = weights.shape
    slots = ncell + 2
    f32, bf16, i32 = jnp.float32, jnp.bfloat16, jnp.int32
    hbm = pl.BlockSpec(memory_space=pltpu.HBM)
    vmem = pl.BlockSpec(memory_space=pltpu.VMEM)
    dma = pltpu.SemaphoreType.DMA
    drag, source = pl.pallas_call(
        functools.partial(kernel, nsec, ncell),
        out_shape=(
            jax.ShapeDtypeStruct((3, beads, lanes), f32),
            jax.ShapeDtypeStruct((cells_dev, 3 * cells), f32),
        ),
        in_specs=[hbm] * 7,
        out_specs=(hbm, hbm),
        scratch_shapes=[
            pltpu.VMEM((cells_dev, width), bf16),
            pltpu.VMEM((3, beads, lanes), f32),
            pltpu.VMEM((beads, lanes), f32),
            pltpu.VMEM((lists, beads), i32),
            pltpu.VMEM((lists, beads), i32),
            pltpu.VMEM((1, beads), i32),
            pltpu.VMEM((3, beads, lanes), f32),
            pltpu.VMEM((cells_dev, 3 * cells), f32),
            pltpu.VMEM((beads, lists * cells, lanes), bf16),
            pltpu.VMEM((cells_dev, 384), bf16),
            pltpu.VMEM((slots, 1, 128), f32),
            pltpu.VMEM((slots, 1, 128), f32),
            pltpu.VMEM((128, slots * beads), bf16),
            pltpu.VMEM((slots, beads, 384), bf16),
            pltpu.VMEM((slots, beads, 384), bf16),
            pltpu.VMEM((lists // 2, beads * 8, 128), f32),
            pltpu.VMEM((beads * 8, lanes), f32),
            pltpu.VMEM((beads * 8, lanes), f32),
            pltpu.VMEM((lists // 2, beads * 8, 128), f32),
            pltpu.VMEM((slots, beads, 256), bf16),
            pltpu.VMEM((slots, beads, 256), bf16),
            dma((7,)), dma((2,)),
            dma((slots,)), dma((slots,)), dma((slots,)),
            dma((slots,)), dma((slots,)), dma((slots,)),
        ],
        compiler_params=pltpu.CompilerParams(
            collective_id=0, has_side_effects=True, vmem_limit_bytes=60 * 1024 * 1024
        ),
    )(
        fluid, bead_vel.transpose(1, 0, 2), bead_diam,
        weights.reshape(beads, lists * cells, lanes),
        tile_owner.T, tile_local.T, tile_count.reshape(1, beads),
    )
    drag, source = pl.pallas_call(
        hand_over,
        out_shape=(
            jax.ShapeDtypeStruct(drag.shape, f32), jax.ShapeDtypeStruct(source.shape, f32),
        ),
        in_specs=[vmem] * 2,
        out_specs=(vmem, vmem),
        compiler_params=pltpu.CompilerParams(vmem_limit_bytes=60 * 1024 * 1024),
    )(drag, source)
    return drag.transpose(1, 0, 2), source


def solution(mesh):
    both = ("sector", "cell")
    in_specs = (
        P(both, None), P(both, None, None), P(both, None), P(both, None, None, None),
        P(both, None), P(both, None), P(both),
    )
    out_specs = (P(both, None, None), P(both, None))
    body = functools.partial(local, mesh.shape["sector"], mesh.shape["cell"])
    return jax.shard_map(body, mesh=mesh, in_specs=in_specs, out_specs=out_specs, check_vma=False)
```
